32 devices in a mesh: groups: 1, train: 16 (over z, y, x), tensor: 2 (over core).
Axes of the slice: x: 2, y: 2, z: 4, core: 2. Of those that a mesh axis runs over, the one named last changes fastest.
Arguments:
- activations: bfloat16 [4096, 28672], P(('groups', 'train'), 'tensor'), may hold values from -6 to 6
- out_grads: bfloat16 [4096, 8192], P(('groups', 'train'), 'tensor'), may hold values from -6 to 6
- basis_in: bfloat16 [256, 28672], P('train', 'tensor'), may hold values from -0.375 to 0.375
- basis_out: bfloat16 [256, 8192], P('train', 'tensor'), may hold values from -0.375 to 0.375
- eigen_in: float32 [28672], P('tensor'), may hold values from 1 to 100
- eigen_out: float32 [8192], P('tensor'), may hold values from 1 to 100
- query_in: bfloat16 [28672, 64], P('tensor'), may hold values from -0.03125 to 0.03125
- query_out: bfloat16 [8192, 64], P('tensor'), may hold values from -0.0625 to 0.0625
- response_ids: int32 [4096], P(('groups', 'train')), may hold values from 0 to 63, as said below
- lengths: int32 [64], P(('groups', 'train')), may hold values from 1 to 127, as said below
- pair_ids: int32 [32], P('groups'), may hold values from 0 to 31, each once
Outputs:
- token_scores: float32 [4096, 8], P(('groups', 'train'), 'tensor')
- pair_scores: float32 [32, 8], P(('groups', 'train'), 'tensor')
The draws below stay inside these ranges and needn't reach their ends.
Inputs may be any that keep to these rules, and one draw needn't show every extreme that they name: `response_ids`: tokens come in pair slots of 128 in a row, slot k holding responses 2 k (the chosen, first) and 2 k + 1 (the rejected): the first lengths[2 k] tokens of slot k carry id 2 k, the others 2 k + 1. lengths[2 k] + lengths[2 k + 1] = 128 for every slot k. `pair_ids`: A permutation of the pairs.
All inputs are finite; a program needn't handle non-finite values.
Results may differ from the reference program's by a relative error of at most 0.0003.
Values may be sent and summed in bfloat16 or wider, within the bound.
A program may use at most 64 MiB of HBM per device.

```python
import math
import jax
import jax.numpy as jnp
from jax import lax

D = 8192
FF = 28672
BLOCK_IN = 256
BLOCK_OUT = 256
RANK = 8
QUERIES = 8
RESP_LEN = 64
TOKENS = 4096
PAIRS = 32
RESP = 64
FACTORS = 64


def pair_split(key):
    drawn = jax.random.randint(jax.random.fold_in(key, 11), (PAIRS,), 1, 2 * RESP_LEN)
    chosen_pair = jax.random.randint(jax.random.fold_in(key, 12), (), 0, PAIRS)
    return jnp.where(jnp.arange(PAIRS) == chosen_pair, 1, drawn).astype(jnp.int32)


def draw_lengths(key, part):
    first_len = pair_split(key)
    return jnp.stack([first_len, 2 * RESP_LEN - first_len], axis=1).reshape(RESP).astype(jnp.int32)


def draw_response_ids(key, part):
    first_len = pair_split(key)
    position = jnp.arange(TOKENS, dtype=jnp.int32)
    pair_block = position // (2 * RESP_LEN)
    offset_in = position % (2 * RESP_LEN)
    later = (offset_in >= first_len[pair_block]).astype(jnp.int32)
    return (2 * pair_block + later).astype(jnp.int32)


def block_scale(stream_key, dims, split, least, largest):
    level, own = 1.0, jax.random.fold_in(stream_key, 6)
    for dim, parts in split:
        draws = jnp.exp(jax.random.uniform(jax.random.fold_in(own, dim), (parts,), jnp.float32, least / len(split), largest / len(split)))
        level = level * jnp.repeat(draws, dims[dim] // parts).reshape([-1 if axis == dim else 1 for axis in range(len(dims))])
    return level


def bell_draw(key, dims, deviation, most, shards=(), kind=jnp.bfloat16):
    factor_of = block_scale(key, dims, shards, -0.22, 0.18) if shards else 1.0
    values = jax.random.normal(key, dims, jnp.float32) * deviation * factor_of
    return jnp.minimum(jnp.maximum(values, -most), most).astype(kind)


def setup_inputs(seed: int = 0, part: int = 0) -> dict:
    key_list = jax.random.split(jax.random.key(seed), 12)
    part_keys = jax.random.split(jax.random.fold_in(key_list[11], part), 12)
    activations = bell_draw(part_keys[0], (TOKENS, FF), 1.0, 6.0, ((0, 16), (1, 2)))
    out_grads = bell_draw(part_keys[1], (TOKENS, D), 1.0, 6.0, ((0, 16), (1, 2)))
    basis_in = bell_draw(key_list[2], (BLOCK_IN, FF), BLOCK_IN ** -0.5, 0.375, ((0, 16), (1, 2)))
    basis_out = bell_draw(key_list[3], (BLOCK_OUT, D), BLOCK_OUT ** -0.5, 0.375, ((0, 16), (1, 2)))
    eigen_in = jnp.clip(jnp.exp(math.log(100.0) - 4.6051702 * jax.random.uniform(key_list[4], (FF,), jnp.float32) ** block_scale(key_list[4], (FF,), ((0, 2),), -0.2, 0.2)), 1.0, 100.0)
    eigen_out = jnp.clip(jnp.exp(math.log(100.0) - 4.6051702 * jax.random.uniform(key_list[5], (D,), jnp.float32) ** block_scale(key_list[5], (D,), ((0, 2),), -0.2, 0.2)), 1.0, 100.0)
    query_in = bell_draw(key_list[6], (FF, FACTORS), FF ** -0.5, 0.03125, ((0, 2),))
    query_out = bell_draw(key_list[7], (D, FACTORS), D ** -0.5, 0.0625, ((0, 2),))
    response_ids = draw_response_ids(jax.random.fold_in(jax.random.fold_in(key_list[11], part), 71), part)
    lengths = draw_lengths(jax.random.fold_in(jax.random.fold_in(key_list[11], part), 71), part)
    pair_ids = jax.random.permutation(part_keys[10], PAIRS).astype(jnp.int32)
    return dict(activations=activations, out_grads=out_grads, basis_in=basis_in, basis_out=basis_out, eigen_in=eigen_in, eigen_out=eigen_out, query_in=query_in, query_out=query_out, response_ids=response_ids, lengths=lengths, pair_ids=pair_ids)


def fold_side(basis, eigen, query, width_block):
    columns = basis.shape[1]
    blocks = columns // width_block
    basis_full = basis.astype(jnp.float32).reshape(width_block, blocks, width_block)
    scaled = (query.astype(jnp.float32) / eigen[:, None]).reshape(blocks, width_block, query.shape[1])
    folded = jnp.einsum('knj,njm->nkm', basis_full, scaled, precision=lax.Precision.HIGHEST)
    return folded.reshape(columns, query.shape[1])


def reference(activations, out_grads, basis_in, basis_out, eigen_in, eigen_out, query_in, query_out, response_ids, lengths, pair_ids):
    folded_in = fold_side(basis_in, eigen_in, query_in, BLOCK_IN)
    folded_out = fold_side(basis_out, eigen_out, query_out, BLOCK_OUT)
    step_rows = math.gcd(TOKENS, 1024)

    def score_rows(row_pair):
        rows_in, rows_out = row_pair
        proj_in = jnp.dot(rows_in.astype(jnp.float32), folded_in, precision=lax.Precision.HIGHEST)
        proj_out = jnp.dot(rows_out.astype(jnp.float32), folded_out, precision=lax.Precision.HIGHEST)
        return (proj_in * proj_out).reshape(step_rows, QUERIES, RANK).sum(axis=2)

    token_scores = lax.map(score_rows, (activations.reshape(-1, step_rows, FF), out_grads.reshape(-1, step_rows, D)))
    token_scores = token_scores.reshape(TOKENS, QUERIES)
    resp_sums = jax.ops.segment_sum(token_scores, response_ids, num_segments=RESP)
    averages = resp_sums / lengths.astype(jnp.float32)[:, None]
    slot_values = averages[0::2] - averages[1::2]
    pair_scores = jnp.zeros((PAIRS, QUERIES), jnp.float32).at[pair_ids].set(slot_values)
    return token_scores, pair_scores
```

```python
import functools

import jax
import jax.numpy as jnp
from jax import lax
from jax.experimental import pallas as pl
from jax.experimental.pallas import tpu as pltpu
from jax.sharding import PartitionSpec as P

MESH = pl.DeviceIdType.MESH

BLOCK_IN = 256
BLOCK_OUT = 256
RANK = 8
QUERIES = 8


def apply_fn(token_rows, fetched):
    return jnp.einsum(
        "tnk,nkm->tm",
        token_rows,
        fetched,
        precision=lax.Precision.HIGHEST,
        preferred_element_type=jnp.float32,
    )


def fold_local(basis, eigen, query, blocks, block_order):
    own_rows = basis.shape[0]
    scaled = (query.astype(jnp.float32) / eigen[:, None]).reshape(
        blocks, block_order, query.shape[1]
    )
    basis_part = basis.astype(jnp.float32).reshape(own_rows, blocks, block_order)
    return jnp.einsum("knj,njm->nkm", basis_part, scaled, precision=lax.Precision.HIGHEST)


def shards(
    activations,
    out_grads,
    basis_in,
    basis_out,
    eigen_in,
    eigen_out,
    query_in,
    query_out,
    response_ids,
    lengths,
    pair_ids,
):
    tok_rows = activations.shape[0]
    hidden_cols = activations.shape[1]
    feature_cols = out_grads.shape[1]
    blocks_in = hidden_cols // BLOCK_IN
    blocks_out = feature_cols // BLOCK_OUT
    rows_in = activations.reshape(tok_rows, blocks_in, BLOCK_IN)
    rows_out = out_grads.reshape(tok_rows, blocks_out, BLOCK_OUT)
    folded_in = fold_local(basis_in, eigen_in, query_in, blocks_in, BLOCK_IN)
    folded_out = fold_local(basis_out, eigen_out, query_out, blocks_out, BLOCK_OUT)
    proj_in = apply_fn(rows_in, lax.all_gather(folded_in, "train", axis=1, tiled=True))
    proj_out = apply_fn(rows_out, lax.all_gather(folded_out, "train", axis=1, tiled=True))
    proj_in, proj_out = lax.psum((proj_in, proj_out), "tensor")
    scores = (proj_in * proj_out).reshape(tok_rows, QUERIES, RANK).sum(axis=2)
    per_device = QUERIES // lax.axis_size("tensor")
    scores = lax.dynamic_slice_in_dim(scores, lax.axis_index("tensor") * per_device, per_device, 1)
    resp_dev = lengths.shape[0]
    local_ids = response_ids - lax.axis_index("train") * resp_dev
    member = (local_ids[None, :] == jnp.arange(resp_dev, dtype=jnp.int32)[:, None]).astype(
        jnp.float32
    )
    resp_sums = jnp.dot(member, scores, precision=lax.Precision.HIGHEST)
    averages = resp_sums / lengths.astype(jnp.float32)[:, None]
    slot_values = averages[0::2] - averages[1::2]
    every_slot = lax.all_gather(slot_values, "train", axis=0, tiled=True)
    pair_dev = slot_values.shape[0]
    own_pairs = lax.axis_index("train") * pair_dev + jnp.arange(pair_dev, dtype=jnp.int32)
    selector = (pair_ids[None, :] == own_pairs[:, None]).astype(jnp.float32)
    pair_scores = jnp.dot(selector, every_slot, precision=lax.Precision.HIGHEST)
    return (scores, pair_scores)


SHARE = 16
DEPTH = 4
CHUNKS = 4


def fused_kernel(
    act_hbm,
    grad_hbm,
    basis_in_hbm,
    basis_out_hbm,
    eigen_in_hbm,
    eigen_out_hbm,
    query_in_hbm,
    query_out_hbm,
    ids_ref,
    lengths_ref,
    pair_ids_ref,
    scores_ref,
    pairs_ref,
    rows,
    basis,
    eigen,
    query,
    fold,
    proj,
    other,
    slots,
    local_sem,
    send_sem,
    z_sem,
    x_sem,
    y_sem,
    xd_sem,
    yd_sem,
    proj_sem,
    slot_send,
    slot_recv,
):
    me = lax.axis_index("train")
    core = lax.axis_index("tensor")
    x, y, z = lax.rem(me, 2), lax.rem(me // 2, 2), me // 4
    x_side = me + 1 - 2 * x
    y_side = me + 2 - 4 * y
    corner = me + 3 - 2 * x - 4 * y
    partner = 1 - core
    hidden = act_hbm.shape[1]
    total = rows.shape[1]
    blocks_in = hidden // BLOCK_IN
    blocks = total // BLOCK_IN
    per_chunk = blocks // CHUNKS
    half = CHUNKS // 2

    barrier = pltpu.get_barrier_semaphore()
    for step in range(1, SHARE):
        pl.semaphore_signal(
            barrier, inc=1, device_id={"train": lax.rem(me + step, SHARE)}, device_id_type=MESH
        )
    pl.semaphore_signal(barrier, inc=1, device_id={"tensor": partner}, device_id_type=MESH)

    first, second = pl.ds(0, hidden), pl.ds(hidden, total - hidden)
    loads = []
    pairs = [
        (basis_in_hbm, basis.at[:, first]),
        (basis_out_hbm, basis.at[:, second]),
        (eigen_in_hbm, eigen.at[:, first]),
        (eigen_out_hbm, eigen.at[:, second]),
        (query_in_hbm, query.at[pl.ds(0, 64), first]),
        (query_out_hbm, query.at[pl.ds(0, 64), second]),
        (query_in_hbm, query.at[pl.ds(64, 64), first]),
        (query_out_hbm, query.at[pl.ds(64, 64), second]),
        (act_hbm, rows.at[:, first]),
        (grad_hbm, rows.at[:, second]),
    ]
    for i, (a, b) in enumerate(pairs):
        loads.append(pltpu.make_async_copy(a, b, local_sem.at[i]))
    for load in loads[:8]:
        load.start()
    for load in loads[:8]:
        load.wait()
    for load in loads[8:]:
        load.start()

    low_lanes = lax.broadcasted_iota(jnp.int32, (16, 128), 1) >= 64

    def fold_block(b, carry):
        cols = pl.ds(pl.multiple_of(b * BLOCK_IN, BLOCK_IN), BLOCK_IN)
        scaled = basis[:, cols].astype(jnp.float32) * (1.0 / eigen[:, cols])
        high = scaled.astype(jnp.bfloat16)
        low = (scaled - high.astype(jnp.float32)).astype(jnp.bfloat16)
        weights = query[:, cols]
        dims = (((1,), (1,)), ((), ()))
        both = lax.dot_general(
            jnp.concatenate([high, low], axis=0), weights, dims, preferred_element_type=jnp.float32
        )
        folded = both[:16] + both[16:]
        top = folded.astype(jnp.bfloat16).astype(jnp.float32)
        fold[me, b] = jnp.where(low_lanes, folded - top, top).astype(jnp.bfloat16)
        return carry

    pending = []

    def copy_of(origin, chunk, index, sem, target):
        ref = fold.at[origin, pl.ds(chunk * per_chunk, per_chunk)]
        return pltpu.make_async_remote_copy(
            src_ref=ref,
            dst_ref=ref,
            send_sem=send_sem.at[index],
            recv_sem=sem,
            device_id={"train": target},
            device_id_type=MESH,
        )

    def send(when, origin, chunk, sem, target):
        copy = copy_of(origin, chunk, len(pending), sem, target)
        pending.append(((when,), chunk))
        copy.start()

    def send_if(when, cond, origin, chunk, sem, target):
        copy = copy_of(origin, chunk, len(pending), sem, target)
        pending.append(((when, cond), chunk))

        @pl.when(cond)
        def _():
            copy.start()

    def arrived(origin, chunk, sem):
        copy_of(origin, chunk, 0, sem, x_side).wait_recv()

    always = z >= 0
    up, down = z < DEPTH - 1, z > 0

    for chunk in range(CHUNKS):
        lax.fori_loop(chunk * per_chunk, (chunk + 1) * per_chunk, fold_block, 0, unroll=6)
        if chunk == 0:
            pl.semaphore_wait(barrier, SHARE)
        send_if(always, up, me, chunk, z_sem.at[0, 0, chunk], me + 4)
        send_if(always, down, me, chunk, z_sem.at[1, 0, chunk], me - 4)
        send(always, me, chunk, x_sem.at[z, chunk], x_side)
        send(always, me, chunk, y_sem.at[z, chunk], y_side)

    def column(step):
        for chunk in range(CHUNKS):
            for way, shift in ((0, -step), (1, step)):
                when = z + shift >= 0 if shift < 0 else z + shift < DEPTH

                @pl.when(when)
                def _():
                    origin = me + 4 * shift
                    arrived(origin, chunk, z_sem.at[way, step - 1, chunk])
                    if step < DEPTH - 1:
                        cond, target = (up, me + 4) if way == 0 else (down, me - 4)
                        send_if(when, cond, origin, chunk, z_sem.at[way, step, chunk], target)
                    send(when, origin, chunk, x_sem.at[z + shift, chunk], x_side)
                    send(when, origin, chunk, y_sem.at[z + shift, chunk], y_side)

    def across(step):
        shifts = (0,) if step == 0 else (-step, step)
        for chunk in range(half):
            for shift in shifts:
                when = z + shift >= 0 if shift < 0 else z + shift < DEPTH

                @pl.when(when)
                def _():
                    level = z + shift
                    origin = x_side + 4 * shift
                    arrived(origin, chunk, x_sem.at[level, chunk])
                    send(when, origin, chunk, yd_sem.at[level, chunk], y_side)
                    origin = y_side + 4 * shift
                    arrived(origin, half + chunk, y_sem.at[level, half + chunk])
                    send(when, origin, half + chunk, xd_sem.at[level, chunk], x_side)

    column(1)
    across(0)
    column(2)
    across(1)
    column(3)
    across(2)
    across(3)

    for load in loads[8:]:
        load.wait()
    for level in range(DEPTH):
        shift = 4 * (level - z)
        for chunk in range(half):
            arrived(x_side + shift, half + chunk, x_sem.at[level, half + chunk])
            arrived(y_side + shift, chunk, y_sem.at[level, chunk])
            arrived(corner + shift, chunk, yd_sem.at[level, chunk])
            arrived(corner + shift, half + chunk, xd_sem.at[level, chunk])

    def apply_block(b, acc):
        cols = pl.ds(pl.multiple_of(b * BLOCK_IN, BLOCK_IN), BLOCK_IN)
        weights = fold[:, b].reshape(BLOCK_IN, 128)
        return acc + jnp.dot(rows[:, cols], weights, preferred_element_type=jnp.float32)

    zero = jnp.zeros((rows.shape[0], 128), jnp.float32)
    for side, (start, stop) in enumerate(((0, blocks_in), (blocks_in, blocks))):
        acc = lax.fori_loop(start, stop, apply_block, zero, unroll=8)
        turned = acc.T
        summed = turned[:64] + turned[64:]
        proj[0, side] = summed[:32]
        proj[1, side] = summed[32:]
    swap = pltpu.make_async_remote_copy(
        src_ref=proj.at[partner],
        dst_ref=other,
        send_sem=proj_sem.at[0],
        recv_sem=proj_sem.at[1],
        device_id={"tensor": partner},
        device_id_type=MESH,
    )
    swap.start()

    tokens = rows.shape[0]
    own_ids = ids_ref[...] - me * 4
    signs = []
    for slot in range(2):
        weight = jnp.zeros((1, tokens), jnp.float32)
        for k, sign in ((2 * slot, 1.0), (2 * slot + 1, -1.0)):
            count = jnp.full((1, tokens), lengths_ref[k], jnp.int32).astype(jnp.float32)
            weight = weight + jnp.where(own_ids == k, sign / count, 0.0)
        signs.append(weight)

    swap.wait()
    full = proj[core] + other[...]
    scores = (full[0] * full[1]).reshape(4, RANK, tokens).sum(axis=1)
    scores_ref[...] = scores
    parts = [
        jnp.broadcast_to(jnp.sum(scores * weight, axis=1, keepdims=True), (4, 128))
        for weight in signs
    ]
    slots[me] = jnp.concatenate(parts, axis=0)

    def slot_copy(step):
        target = lax.rem(me + step, SHARE)
        return pltpu.make_async_remote_copy(
            src_ref=slots.at[me],
            dst_ref=slots.at[me],
            send_sem=slot_send.at[step],
            recv_sem=slot_recv.at[step],
            device_id={"train": target},
            device_id_type=MESH,
        )

    for step in range(1, SHARE):
        slot_copy(step).start()
    for index, (conds, chunk) in enumerate(pending):

        @pl.when(functools.reduce(jnp.logical_and, conds))
        def _():
            copy_of(me, chunk, index, x_sem.at[0, 0], x_side).wait_send()

    for step in range(1, SHARE):
        origin = lax.rem(me + SHARE - step, SHARE)
        pltpu.make_async_remote_copy(
            src_ref=slots.at[origin],
            dst_ref=slots.at[origin],
            send_sem=slot_send.at[step],
            recv_sem=slot_recv.at[step],
            device_id={"train": origin},
            device_id_type=MESH,
        ).wait_recv()
        slot_copy(step).wait_send()

    row = lax.broadcasted_iota(jnp.int32, (4, 128), 0)
    lane = lax.broadcasted_iota(jnp.int32, (4, 128), 1)
    for own in range(2):
        value = jnp.zeros((4, 128), jnp.float32)
        for k in range(2 * SHARE):
            same = jnp.full((4, 128), pair_ids_ref[k], jnp.int32) == me * 2 + own
            value = value + jnp.where(same, slots[k // 2, 4 * (k % 2) : 4 * (k % 2) + 4], 0.0)
        line = jnp.sum(jnp.where(row == lane, value, 0.0), axis=0, keepdims=True)
        pairs_ref[own : own + 1] = line[:, :4]


def fused(
    activations,
    out_grads,
    basis_in,
    basis_out,
    eigen_in,
    eigen_out,
    query_in,
    query_out,
    response_ids,
    lengths,
    pair_ids,
):
    tokens, hidden = activations.shape
    total = hidden + out_grads.shape[1]
    blocks = total // BLOCK_IN
    share = basis_in.shape[0]
    vmem = pl.BlockSpec(memory_space=pltpu.VMEM)
    smem = pl.BlockSpec(memory_space=pltpu.SMEM)
    scores, pair_scores = pl.pallas_call(
        fused_kernel,
        out_shape=(
            jax.ShapeDtypeStruct((4, tokens), jnp.float32),
            jax.ShapeDtypeStruct((2, 4), jnp.float32),
        ),
        in_specs=[pl.BlockSpec(memory_space=pl.ANY)] * 8 + [vmem, smem, smem],
        out_specs=(vmem, vmem),
        scratch_shapes=[
            pltpu.VMEM((tokens, total), jnp.bfloat16),
            pltpu.VMEM((share, total), jnp.bfloat16),
            pltpu.VMEM((1, total), jnp.float32),
            pltpu.VMEM((128, total), jnp.bfloat16),
            pltpu.VMEM((SHARE, blocks, share, 128), jnp.bfloat16),
            pltpu.VMEM((2, 2, 32, tokens), jnp.float32),
            pltpu.VMEM((2, 32, tokens), jnp.float32),
            pltpu.VMEM((SHARE, 8, 128), jnp.float32),
            pltpu.SemaphoreType.DMA((10,)),
            pltpu.SemaphoreType.DMA((40 * CHUNKS,)),
            pltpu.SemaphoreType.DMA((2, DEPTH - 1, CHUNKS)),
            pltpu.SemaphoreType.DMA((DEPTH, CHUNKS)),
            pltpu.SemaphoreType.DMA((DEPTH, CHUNKS)),
            pltpu.SemaphoreType.DMA((DEPTH, CHUNKS // 2)),
            pltpu.SemaphoreType.DMA((DEPTH, CHUNKS // 2)),
            pltpu.SemaphoreType.DMA((2,)),
            pltpu.SemaphoreType.DMA((SHARE,)),
            pltpu.SemaphoreType.DMA((SHARE,)),
        ],
        compiler_params=pltpu.CompilerParams(
            collective_id=0, has_side_effects=True, vmem_limit_bytes=48 * 1024 * 1024
        ),
    )(
        activations,
        out_grads,
        basis_in,
        basis_out,
        eigen_in.reshape(1, -1),
        eigen_out.reshape(1, -1),
        query_in.T,
        query_out.T,
        response_ids.reshape(1, -1),
        lengths,
        pair_ids,
    )
    return scores.T, pair_scores


def solution(mesh):
    sizes = (mesh.shape["groups"], mesh.shape["train"], mesh.shape["tensor"])
    body = fused if sizes == (1, 16, 2) else shards
    return jax.shard_map(
        body,
        mesh=mesh,
        in_specs=(
            P(("groups", "train"), "tensor"),
            P(("groups", "train"), "tensor"),
            P("train", "tensor"),
            P("train", "tensor"),
            P("tensor"),
            P("tensor"),
            P("tensor", None),
            P("tensor", None),
            P(("groups", "train")),
            P(("groups", "train")),
            P("groups"),
        ),
        out_specs=(P(("groups", "train"), "tensor"), P(("groups", "train"), "tensor")),
        check_vma=False,
    )
```

```python
import functools

import jax
import jax.numpy as jnp
from jax import lax
from jax.experimental import pallas as pl
from jax.experimental.pallas import tpu as pltpu
from jax.sharding import PartitionSpec as P

MESH = pl.DeviceIdType.MESH

BLOCK_IN = 256
BLOCK_OUT = 256
RANK = 8
QUERIES = 8


def apply_fn(token_rows, fetched):
    return jnp.einsum(
        "tnk,nkm->tm",
        token_rows,
        fetched,
        precision=lax.Precision.HIGHEST,
        preferred_element_type=jnp.float32,
    )


def fold_local(basis, eigen, query, blocks, block_order):
    own_rows = basis.shape[0]
    scaled = (query.astype(jnp.float32) / eigen[:, None]).reshape(
        blocks, block_order, query.shape[1]
    )
    basis_part = basis.astype(jnp.float32).reshape(own_rows, blocks, block_order)
    return jnp.einsum("knj,njm->nkm", basis_part, scaled, precision=lax.Precision.HIGHEST)


def shards(
    activations,
    out_grads,
    basis_in,
    basis_out,
    eigen_in,
    eigen_out,
    query_in,
    query_out,
    response_ids,
    lengths,
    pair_ids,
):
    tok_rows = activations.shape[0]
    hidden_cols = activations.shape[1]
    feature_cols = out_grads.shape[1]
    blocks_in = hidden_cols // BLOCK_IN
    blocks_out = feature_cols // BLOCK_OUT
    rows_in = activations.reshape(tok_rows, blocks_in, BLOCK_IN)
    rows_out = out_grads.reshape(tok_rows, blocks_out, BLOCK_OUT)
    folded_in = fold_local(basis_in, eigen_in, query_in, blocks_in, BLOCK_IN)
    folded_out = fold_local(basis_out, eigen_out, query_out, blocks_out, BLOCK_OUT)
    proj_in = apply_fn(rows_in, lax.all_gather(folded_in, "train", axis=1, tiled=True))
    proj_out = apply_fn(rows_out, lax.all_gather(folded_out, "train", axis=1, tiled=True))
    proj_in, proj_out = lax.psum((proj_in, proj_out), "tensor")
    scores = (proj_in * proj_out).reshape(tok_rows, QUERIES, RANK).sum(axis=2)
    per_device = QUERIES // lax.axis_size("tensor")
    scores = lax.dynamic_slice_in_dim(scores, lax.axis_index("tensor") * per_device, per_device, 1)
    resp_dev = lengths.shape[0]
    local_ids = response_ids - lax.axis_index("train") * resp_dev
    member = (local_ids[None, :] == jnp.arange(resp_dev, dtype=jnp.int32)[:, None]).astype(
        jnp.float32
    )
    resp_sums = jnp.dot(member, scores, precision=lax.Precision.HIGHEST)
    averages = resp_sums / lengths.astype(jnp.float32)[:, None]
    slot_values = averages[0::2] - averages[1::2]
    every_slot = lax.all_gather(slot_values, "train", axis=0, tiled=True)
    pair_dev = slot_values.shape[0]
    own_pairs = lax.axis_index("train") * pair_dev + jnp.arange(pair_dev, dtype=jnp.int32)
    selector = (pair_ids[None, :] == own_pairs[:, None]).astype(jnp.float32)
    pair_scores = jnp.dot(selector, every_slot, precision=lax.Precision.HIGHEST)
    return (scores, pair_scores)


SHARE = 16
DEPTH = 4
CHUNKS = 2
GROUP = 2


def fused_kernel(
    act_hbm,
    grad_hbm,
    basis_in_hbm,
    basis_out_hbm,
    eigen_in_hbm,
    eigen_out_hbm,
    query_in_hbm,
    query_out_hbm,
    ids_ref,
    lengths_ref,
    pair_ids_ref,
    scores_ref,
    pairs_ref,
    rows,
    basis,
    eigen,
    query,
    fold,
    scales,
    proj,
    other,
    slots,
    local_sem,
    send_sem,
    z_sem,
    x_sem,
    y_sem,
    xd_sem,
    yd_sem,
    proj_sem,
    slot_send,
    slot_recv,
):
    me = lax.axis_index("train")
    core = lax.axis_index("tensor")
    x, y, z = lax.rem(me, 2), lax.rem(me // 2, 2), me // 4
    x_side = me + 1 - 2 * x
    y_side = me + 2 - 4 * y
    corner = me + 3 - 2 * x - 4 * y
    partner = 1 - core
    hidden = act_hbm.shape[1]
    total = rows.shape[1]
    blocks_in = hidden // BLOCK_IN
    blocks = total // BLOCK_IN
    half_blocks = blocks // 2
    data = half_blocks // CHUNKS
    per_chunk = data + 1
    half = CHUNKS // 2

    barrier = pltpu.get_barrier_semaphore()
    for step in range(1, SHARE):
        pl.semaphore_signal(
            barrier, inc=1, device_id={"train": lax.rem(me + step, SHARE)}, device_id_type=MESH
        )
    pl.semaphore_signal(barrier, inc=1, device_id={"tensor": partner}, device_id_type=MESH)

    first, second = pl.ds(0, hidden), pl.ds(hidden, total - hidden)
    loads = []
    pairs = [
        (basis_in_hbm, basis.at[:, first]),
        (basis_out_hbm, basis.at[:, second]),
        (eigen_in_hbm, eigen.at[:, first]),
        (eigen_out_hbm, eigen.at[:, second]),
        (query_in_hbm, query.at[pl.ds(0, 64), first]),
        (query_out_hbm, query.at[pl.ds(0, 64), second]),
        (query_in_hbm, query.at[pl.ds(64, 64), first]),
        (query_out_hbm, query.at[pl.ds(64, 64), second]),
        (act_hbm, rows.at[:, first]),
        (grad_hbm, rows.at[:, second]),
    ]
    for i, (a, b) in enumerate(pairs):
        loads.append(pltpu.make_async_copy(a, b, local_sem.at[i]))
    for load in loads[:8]:
        load.start()
    for load in loads[:8]:
        load.wait()
    for load in loads[8:]:
        load.start()

    upper = lax.broadcasted_iota(jnp.int32, (16, 128), 1) >= 64
    row_of = lax.broadcasted_iota(jnp.int32, (16, 128), 0)

    def fold_block(b):
        cols = pl.ds(pl.multiple_of(b * BLOCK_IN, BLOCK_IN), BLOCK_IN)
        scaled = basis[:, cols].astype(jnp.float32) * (1.0 / eigen[:, cols])
        high = scaled.astype(jnp.bfloat16)
        low = (scaled - high.astype(jnp.float32)).astype(jnp.bfloat16)
        dims = (((1,), (1,)), ((), ()))
        both = lax.dot_general(
            jnp.concatenate([high, low], axis=0),
            query[:, cols],
            dims,
            preferred_element_type=jnp.float32,
        )
        return both[:16] + both[16:]

    def fold_group(chunk, r, exponents):
        values = []
        for i in range(GROUP):
            b = chunk * data + r * GROUP + i
            values.append(jnp.where(upper, fold_block(b + half_blocks), fold_block(b)))
        largest = functools.reduce(jnp.maximum, [jnp.abs(v) for v in values])
        largest = jnp.maximum(jnp.max(largest, axis=0, keepdims=True), 1e-30)
        exponent = jnp.floor(jnp.log2(largest)) - 14.0
        inverse = jnp.exp2(-exponent)
        for i, v in enumerate(values):
            steps = jnp.clip(jnp.round(v * inverse), -32767.0, 32767.0)
            tile = chunk * per_chunk + r * GROUP + i
            fold[me, tile] = steps.astype(jnp.int32).astype(jnp.int16)
        return jnp.where(row_of == r, exponent, exponents)

    pending = []

    def copy_of(origin, chunk, index, sem, target):
        ref = fold.at[origin, pl.ds(chunk * per_chunk, per_chunk)]
        return pltpu.make_async_remote_copy(
            src_ref=ref,
            dst_ref=ref,
            send_sem=send_sem.at[index],
            recv_sem=sem,
            device_id={"train": target},
            device_id_type=MESH,
        )

    def send(when, origin, chunk, sem, target):
        copy = copy_of(origin, chunk, len(pending), sem, target)
        pending.append(((when,), chunk))
        copy.start()

    def send_if(when, cond, origin, chunk, sem, target):
        copy = copy_of(origin, chunk, len(pending), sem, target)
        pending.append(((when, cond), chunk))

        @pl.when(cond)
        def _():
            copy.start()

    def arrived(origin, chunk, sem):
        copy_of(origin, chunk, 0, sem, x_side).wait_recv()

    always = z >= 0
    up, down = z < DEPTH - 1, z > 0

    for chunk in range(CHUNKS):
        exponents = lax.fori_loop(
            0,
            data // GROUP,
            functools.partial(fold_group, chunk),
            jnp.zeros((16, 128), jnp.float32),
            unroll=3,
        )
        fold[me, chunk * per_chunk + data] = exponents.astype(jnp.int32).astype(jnp.int16)
        if chunk == 0:
            pl.semaphore_wait(barrier, SHARE)
        send_if(always, up, me, chunk, z_sem.at[0, 0, chunk], me + 4)
        send_if(always, down, me, chunk, z_sem.at[1, 0, chunk], me - 4)
        send(always, me, chunk, x_sem.at[z, chunk], x_side)
        send(always, me, chunk, y_sem.at[z, chunk], y_side)

    def column(step):
        for chunk in range(CHUNKS):
            for way, shift in ((0, -step), (1, step)):
                when = z + shift >= 0 if shift < 0 else z + shift < DEPTH

                @pl.when(when)
                def _():
                    origin = me + 4 * shift
                    arrived(origin, chunk, z_sem.at[way, step - 1, chunk])
                    if step < DEPTH - 1:
                        cond, target = (up, me + 4) if way == 0 else (down, me - 4)
                        send_if(when, cond, origin, chunk, z_sem.at[way, step, chunk], target)
                    send(when, origin, chunk, x_sem.at[z + shift, chunk], x_side)
                    send(when, origin, chunk, y_sem.at[z + shift, chunk], y_side)

    def across(step):
        shifts = (0,) if step == 0 else (-step, step)
        for chunk in range(half):
            for shift in shifts:
                when = z + shift >= 0 if shift < 0 else z + shift < DEPTH

                @pl.when(when)
                def _():
                    level = z + shift
                    origin = x_side + 4 * shift
                    arrived(origin, chunk, x_sem.at[level, chunk])
                    send(when, origin, chunk, yd_sem.at[level, chunk], y_side)
                    origin = y_side + 4 * shift
                    arrived(origin, half + chunk, y_sem.at[level, half + chunk])
                    send(when, origin, half + chunk, xd_sem.at[level, chunk], x_side)

    column(1)
    across(0)
    column(2)
    across(1)
    column(3)
    across(2)
    across(3)

    for load in loads[8:]:
        load.wait()
    for level in range(DEPTH):
        shift = 4 * (level - z)
        for chunk in range(half):
            arrived(x_side + shift, half + chunk, x_sem.at[level, half + chunk])
            arrived(y_side + shift, chunk, y_sem.at[level, chunk])
            arrived(corner + shift, chunk, yd_sem.at[level, chunk])
            arrived(corner + shift, half + chunk, xd_sem.at[level, chunk])

    for chunk in range(CHUNKS):
        for origin in range(SHARE):
            held = fold[origin, chunk * per_chunk + data].astype(jnp.int32).astype(jnp.float32)
            scales[chunk, origin] = jnp.exp2(held)

    wide = lax.broadcasted_iota(jnp.int32, (BLOCK_IN, 128), 1) >= 64

    def parts_of(folded):
        top = folded.astype(jnp.bfloat16).astype(jnp.float32)
        return jnp.where(wide, folded - top, top).astype(jnp.bfloat16)

    def apply_pair(p, carry):
        acc_one, acc_two = carry
        chunk = p // data
        group = lax.rem(p, data) // GROUP
        steps = fold[:, p + chunk].astype(jnp.int32).astype(jnp.float32)
        values = (steps * scales[chunk, :, pl.ds(group, 1), :]).reshape(BLOCK_IN, 128)
        turned = pltpu.roll(values, 64, 1)
        one = parts_of(jnp.where(wide, turned, values))
        two = parts_of(jnp.where(wide, values, turned))
        cols = pl.ds(pl.multiple_of(p * BLOCK_IN, BLOCK_IN), BLOCK_IN)
        acc_one = acc_one + jnp.dot(rows[:, cols], one, preferred_element_type=jnp.float32)
        cols = pl.ds(pl.multiple_of((p + half_blocks) * BLOCK_IN, BLOCK_IN), BLOCK_IN)
        acc_two = acc_two + jnp.dot(rows[:, cols], two, preferred_element_type=jnp.float32)
        return acc_one, acc_two

    zero = jnp.zeros((rows.shape[0], 128), jnp.float32)
    split = blocks_in - half_blocks
    acc_one, acc_two = lax.fori_loop(0, split, apply_pair, (zero, zero), unroll=4)
    sums_in = acc_one + acc_two
    sums_in, sums_out = lax.fori_loop(split, half_blocks, apply_pair, (sums_in, zero), unroll=4)
    for side, acc in enumerate((sums_in, sums_out)):
        turned = acc.T
        summed = turned[:64] + turned[64:]
        proj[0, side] = summed[:32]
        proj[1, side] = summed[32:]
    swap = pltpu.make_async_remote_copy(
        src_ref=proj.at[partner],
        dst_ref=other,
        send_sem=proj_sem.at[0],
        recv_sem=proj_sem.at[1],
        device_id={"tensor": partner},
        device_id_type=MESH,
    )
    swap.start()

    tokens = rows.shape[0]
    own_ids = ids_ref[...] - me * 4
    signs = []
    for slot in range(2):
        weight = jnp.zeros((1, tokens), jnp.float32)
        for k, sign in ((2 * slot, 1.0), (2 * slot + 1, -1.0)):
            count = jnp.full((1, tokens), lengths_ref[k], jnp.int32).astype(jnp.float32)
            weight = weight + jnp.where(own_ids == k, sign / count, 0.0)
        signs.append(weight)

    swap.wait()
    full = proj[core] + other[...]
    scores = (full[0] * full[1]).reshape(4, RANK, tokens).sum(axis=1)
    scores_ref[...] = scores
    parts = [
        jnp.broadcast_to(jnp.sum(scores * weight, axis=1, keepdims=True), (4, 128))
        for weight in signs
    ]
    slots[me] = jnp.concatenate(parts, axis=0)

    def slot_copy(step):
        target = lax.rem(me + step, SHARE)
        return pltpu.make_async_remote_copy(
            src_ref=slots.at[me],
            dst_ref=slots.at[me],
            send_sem=slot_send.at[step],
            recv_sem=slot_recv.at[step],
            device_id={"train": target},
            device_id_type=MESH,
        )

    for step in range(1, SHARE):
        slot_copy(step).start()
    for index, (conds, chunk) in enumerate(pending):

        @pl.when(functools.reduce(jnp.logical_and, conds))
        def _():
            copy_of(me, chunk, index, x_sem.at[0, 0], x_side).wait_send()

    for step in range(1, SHARE):
        origin = lax.rem(me + SHARE - step, SHARE)
        pltpu.make_async_remote_copy(
            src_ref=slots.at[origin],
            dst_ref=slots.at[origin],
            send_sem=slot_send.at[step],
            recv_sem=slot_recv.at[step],
            device_id={"train": origin},
            device_id_type=MESH,
        ).wait_recv()
        slot_copy(step).wait_send()

    row = lax.broadcasted_iota(jnp.int32, (4, 128), 0)
    lane = lax.broadcasted_iota(jnp.int32, (4, 128), 1)
    for own in range(2):
        value = jnp.zeros((4, 128), jnp.float32)
        for k in range(2 * SHARE):
            same = jnp.full((4, 128), pair_ids_ref[k], jnp.int32) == me * 2 + own
            value = value + jnp.where(same, slots[k // 2, 4 * (k % 2) : 4 * (k % 2) + 4], 0.0)
        line = jnp.sum(jnp.where(row == lane, value, 0.0), axis=0, keepdims=True)
        pairs_ref[own : own + 1] = line[:, :4]


def fused(
    activations,
    out_grads,
    basis_in,
    basis_out,
    eigen_in,
    eigen_out,
    query_in,
    query_out,
    response_ids,
    lengths,
    pair_ids,
):
    tokens, hidden = activations.shape
    total = hidden + out_grads.shape[1]
    blocks = total // BLOCK_IN
    share = basis_in.shape[0]
    vmem = pl.BlockSpec(memory_space=pltpu.VMEM)
    smem = pl.BlockSpec(memory_space=pltpu.SMEM)
    scores, pair_scores = pl.pallas_call(
        fused_kernel,
        out_shape=(
            jax.ShapeDtypeStruct((4, tokens), jnp.float32),
            jax.ShapeDtypeStruct((2, 4), jnp.float32),
        ),
        in_specs=[pl.BlockSpec(memory_space=pl.ANY)] * 8 + [vmem, smem, smem],
        out_specs=(vmem, vmem),
        scratch_shapes=[
            pltpu.VMEM((tokens, total), jnp.bfloat16),
            pltpu.VMEM((share, total), jnp.bfloat16),
            pltpu.VMEM((1, total), jnp.float32),
            pltpu.VMEM((128, total), jnp.bfloat16),
            pltpu.VMEM((SHARE, blocks // 2 + CHUNKS, share, 128), jnp.int16),
            pltpu.VMEM((CHUNKS, SHARE, share, 128), jnp.float32),
            pltpu.VMEM((2, 2, 32, tokens), jnp.float32),
            pltpu.VMEM((2, 32, tokens), jnp.float32),
            pltpu.VMEM((SHARE, 8, 128), jnp.float32),
            pltpu.SemaphoreType.DMA((10,)),
            pltpu.SemaphoreType.DMA((40 * CHUNKS,)),
            pltpu.SemaphoreType.DMA((2, DEPTH - 1, CHUNKS)),
            pltpu.SemaphoreType.DMA((DEPTH, CHUNKS)),
            pltpu.SemaphoreType.DMA((DEPTH, CHUNKS)),
            pltpu.SemaphoreType.DMA((DEPTH, CHUNKS // 2)),
            pltpu.SemaphoreType.DMA((DEPTH, CHUNKS // 2)),
            pltpu.SemaphoreType.DMA((2,)),
            pltpu.SemaphoreType.DMA((SHARE,)),
            pltpu.SemaphoreType.DMA((SHARE,)),
        ],
        compiler_params=pltpu.CompilerParams(
            collective_id=0, has_side_effects=True, vmem_limit_bytes=60 * 1024 * 1024
        ),
    )(
        activations,
        out_grads,
        basis_in,
        basis_out,
        eigen_in.reshape(1, -1),
        eigen_out.reshape(1, -1),
        query_in.T,
        query_out.T,
        response_ids.reshape(1, -1),
        lengths,
        pair_ids,
    )
    return scores.T, pair_scores


def solution(mesh):
    sizes = (mesh.shape["groups"], mesh.shape["train"], mesh.shape["tensor"])
    body = fused if sizes == (1, 16, 2) else shards
    return jax.shard_map(
        body,
        mesh=mesh,
        in_specs=(
            P(("groups", "train"), "tensor"),
            P(("groups", "train"), "tensor"),
            P("train", "tensor"),
            P("train", "tensor"),
            P("tensor"),
            P("tensor"),
            P("tensor", None),
            P("tensor", None),
            P(("groups", "train")),
            P(("groups", "train")),
            P("groups"),
        ),
        out_specs=(P(("groups", "train"), "tensor"), P(("groups", "train"), "tensor")),
        check_vma=False,
    )
```

```python
import functools

import jax
import jax.numpy as jnp
from jax import lax
from jax.experimental import pallas as pl
from jax.experimental.pallas import tpu as pltpu
from jax.sharding import PartitionSpec as P

MESH = pl.DeviceIdType.MESH

BLOCK_IN = 256
BLOCK_OUT = 256
RANK = 8
QUERIES = 8


def apply_fn(token_rows, fetched):
    return jnp.einsum(
        "tnk,nkm->tm",
        token_rows,
        fetched,
        precision=lax.Precision.HIGHEST,
        preferred_element_type=jnp.float32,
    )


def fold_local(basis, eigen, query, blocks, block_order):
    own_rows = basis.shape[0]
    scaled = (query.astype(jnp.float32) / eigen[:, None]).reshape(
        blocks, block_order, query.shape[1]
    )
    basis_part = basis.astype(jnp.float32).reshape(own_rows, blocks, block_order)
    return jnp.einsum("knj,njm->nkm", basis_part, scaled, precision=lax.Precision.HIGHEST)


def shards(
    activations,
    out_grads,
    basis_in,
    basis_out,
    eigen_in,
    eigen_out,
    query_in,
    query_out,
    response_ids,
    lengths,
    pair_ids,
):
    tok_rows = activations.shape[0]
    hidden_cols = activations.shape[1]
    feature_cols = out_grads.shape[1]
    blocks_in = hidden_cols // BLOCK_IN
    blocks_out = feature_cols // BLOCK_OUT
    rows_in = activations.reshape(tok_rows, blocks_in, BLOCK_IN)
    rows_out = out_grads.reshape(tok_rows, blocks_out, BLOCK_OUT)
    folded_in = fold_local(basis_in, eigen_in, query_in, blocks_in, BLOCK_IN)
    folded_out = fold_local(basis_out, eigen_out, query_out, blocks_out, BLOCK_OUT)
    proj_in = apply_fn(rows_in, lax.all_gather(folded_in, "train", axis=1, tiled=True))
    proj_out = apply_fn(rows_out, lax.all_gather(folded_out, "train", axis=1, tiled=True))
    proj_in, proj_out = lax.psum((proj_in, proj_out), "tensor")
    scores = (proj_in * proj_out).reshape(tok_rows, QUERIES, RANK).sum(axis=2)
    per_device = QUERIES // lax.axis_size("tensor")
    scores = lax.dynamic_slice_in_dim(scores, lax.axis_index("tensor") * per_device, per_device, 1)
    resp_dev = lengths.shape[0]
    local_ids = response_ids - lax.axis_index("train") * resp_dev
    member = (local_ids[None, :] == jnp.arange(resp_dev, dtype=jnp.int32)[:, None]).astype(
        jnp.float32
    )
    resp_sums = jnp.dot(member, scores, precision=lax.Precision.HIGHEST)
    averages = resp_sums / lengths.astype(jnp.float32)[:, None]
    slot_values = averages[0::2] - averages[1::2]
    every_slot = lax.all_gather(slot_values, "train", axis=0, tiled=True)
    pair_dev = slot_values.shape[0]
    own_pairs = lax.axis_index("train") * pair_dev + jnp.arange(pair_dev, dtype=jnp.int32)
    selector = (pair_ids[None, :] == own_pairs[:, None]).astype(jnp.float32)
    pair_scores = jnp.dot(selector, every_slot, precision=lax.Precision.HIGHEST)
    return (scores, pair_scores)


SHARE = 16
DEPTH = 4
CHUNKS = 2
GROUP = 2


def fused_kernel(
    act_hbm,
    grad_hbm,
    basis_in_hbm,
    basis_out_hbm,
    eigen_in_hbm,
    eigen_out_hbm,
    query_in_hbm,
    query_out_hbm,
    ids_ref,
    lengths_ref,
    pair_ids_ref,
    scores_ref,
    pairs_ref,
    rows,
    basis,
    eigen,
    query,
    fold,
    scales,
    proj,
    other,
    slots,
    local_sem,
    send_sem,
    z_sem,
    x_sem,
    y_sem,
    xd_sem,
    yd_sem,
    zc_sem,
    proj_sem,
    slot_send,
    slot_recv,
):
    me = lax.axis_index("train")
    core = lax.axis_index("tensor")
    x, y, z = lax.rem(me, 2), lax.rem(me // 2, 2), me // 4
    x_side = me + 1 - 2 * x
    y_side = me + 2 - 4 * y
    corner = me + 3 - 2 * x - 4 * y
    partner = 1 - core
    hidden = act_hbm.shape[1]
    total = rows.shape[1]
    blocks_in = hidden // BLOCK_IN
    blocks = total // BLOCK_IN
    half_blocks = blocks // 2
    data = half_blocks // CHUNKS
    per_chunk = data + 1
    half = CHUNKS // 2

    barrier = pltpu.get_barrier_semaphore()
    for step in range(1, SHARE):
        pl.semaphore_signal(
            barrier, inc=1, device_id={"train": lax.rem(me + step, SHARE)}, device_id_type=MESH
        )
    pl.semaphore_signal(barrier, inc=1, device_id={"tensor": partner}, device_id_type=MESH)

    first, second = pl.ds(0, hidden), pl.ds(hidden, total - hidden)
    loads = []
    pairs = [
        (basis_in_hbm, basis.at[:, first]),
        (basis_out_hbm, basis.at[:, second]),
        (eigen_in_hbm, eigen.at[:, first]),
        (eigen_out_hbm, eigen.at[:, second]),
        (query_in_hbm, query.at[pl.ds(0, 64), first]),
        (query_out_hbm, query.at[pl.ds(0, 64), second]),
        (query_in_hbm, query.at[pl.ds(64, 64), first]),
        (query_out_hbm, query.at[pl.ds(64, 64), second]),
        (act_hbm, rows.at[:, first]),
        (grad_hbm, rows.at[:, second]),
    ]
    for i, (a, b) in enumerate(pairs):
        loads.append(pltpu.make_async_copy(a, b, local_sem.at[i]))
    for load in loads[:8]:
        load.start()
    for load in loads[:8]:
        load.wait()
    for load in loads[8:]:
        load.start()

    upper = lax.broadcasted_iota(jnp.int32, (16, 128), 1) >= 64
    row_of = lax.broadcasted_iota(jnp.int32, (16, 128), 0)

    def fold_block(b):
        cols = pl.ds(pl.multiple_of(b * BLOCK_IN, BLOCK_IN), BLOCK_IN)
        scaled = basis[:, cols].astype(jnp.float32) * (1.0 / eigen[:, cols])
        high = scaled.astype(jnp.bfloat16)
        low = (scaled - high.astype(jnp.float32)).astype(jnp.bfloat16)
        dims = (((1,), (1,)), ((), ()))
        both = lax.dot_general(
            jnp.concatenate([high, low], axis=0),
            query[:, cols],
            dims,
            preferred_element_type=jnp.float32,
        )
        return both[:16] + both[16:]

    def fold_group(chunk, r, exponents):
        values = []
        for i in range(GROUP):
            b = chunk * data + r * GROUP + i
            values.append(jnp.where(upper, fold_block(b + half_blocks), fold_block(b)))
        largest = functools.reduce(jnp.maximum, [jnp.abs(v) for v in values])
        largest = jnp.maximum(jnp.max(largest, axis=0, keepdims=True), 1e-30)
        exponent = jnp.floor(jnp.log2(largest)) - 14.0
        inverse = jnp.exp2(-exponent)
        for i, v in enumerate(values):
            steps = jnp.clip(jnp.round(v * inverse), -32767.0, 32767.0)
            tile = chunk * per_chunk + r * GROUP + i
            fold[me, tile] = steps.astype(jnp.int32).astype(jnp.int16)
        return jnp.where(row_of == r, exponent, exponents)

    pending = []

    def copy_of(origin, chunk, index, sem, target):
        ref = fold.at[origin, pl.ds(chunk * per_chunk, per_chunk)]
        return pltpu.make_async_remote_copy(
            src_ref=ref,
            dst_ref=ref,
            send_sem=send_sem.at[index],
            recv_sem=sem,
            device_id={"train": target},
            device_id_type=MESH,
        )

    def send(when, origin, chunk, sem, target):
        copy = copy_of(origin, chunk, len(pending), sem, target)
        pending.append(((when,), chunk))
        copy.start()

    def send_if(when, cond, origin, chunk, sem, target):
        copy = copy_of(origin, chunk, len(pending), sem, target)
        pending.append(((when, cond), chunk))

        @pl.when(cond)
        def _():
            copy.start()

    def arrived(origin, chunk, sem):
        copy_of(origin, chunk, 0, sem, x_side).wait_recv()

    always = z >= 0
    up, down = z < DEPTH - 1, z > 0

    for chunk in range(CHUNKS):
        exponents = lax.fori_loop(
            0,
            data // GROUP,
            functools.partial(fold_group, chunk),
            jnp.zeros((16, 128), jnp.float32),
            unroll=3,
        )
        fold[me, chunk * per_chunk + data] = exponents.astype(jnp.int32).astype(jnp.int16)
        if chunk == 0:
            pl.semaphore_wait(barrier, SHARE)
        send_if(always, up, me, chunk, z_sem.at[0, 0, chunk], me + 4)
        send_if(always, down, me, chunk, z_sem.at[1, 0, chunk], me - 4)
        send(always, me, chunk, x_sem.at[z, chunk], x_side)
        send(always, me, chunk, y_sem.at[z, chunk], y_side)

    def column(step):
        for chunk in range(CHUNKS):
            for way, shift in ((0, -step), (1, step)):
                when = z + shift >= 0 if shift < 0 else z + shift < DEPTH

                @pl.when(when)
                def _():
                    origin = me + 4 * shift
                    arrived(origin, chunk, z_sem.at[way, step - 1, chunk])
                    if step < DEPTH - 1:
                        cond, target = (up, me + 4) if way == 0 else (down, me - 4)
                        send_if(when, cond, origin, chunk, z_sem.at[way, step, chunk], target)
                    send(when, origin, chunk, x_sem.at[z + shift, chunk], x_side)
                    send(when, origin, chunk, y_sem.at[z + shift, chunk], y_side)

    def across(step):
        shifts = (0,) if step == 0 else (-step, step)
        for chunk in range(half):
            for shift in shifts:
                when = z + shift >= 0 if shift < 0 else z + shift < DEPTH

                @pl.when(when)
                def _():
                    level = z + shift
                    origin = x_side + 4 * shift
                    arrived(origin, chunk, x_sem.at[level, chunk])
                    send(when, origin, chunk, yd_sem.at[level, chunk], y_side)
                    origin = y_side + 4 * shift
                    arrived(origin, half + chunk, y_sem.at[level, half + chunk])
                    send(when, origin, half + chunk, xd_sem.at[level, chunk], x_side)

    def corner_share():
        for chunk in range(CHUNKS):
            if chunk < half:
                arrived(corner, chunk, yd_sem.at[z, chunk])
            else:
                arrived(corner, chunk, xd_sem.at[z, chunk - half])
            send_if(always, up, corner, chunk, zc_sem.at[0, chunk], me + 4)
            send_if(always, down, corner, chunk, zc_sem.at[1, chunk], me - 4)

    column(1)
    across(0)
    column(2)
    corner_share()
    column(3)
    across(2)
    across(3)

    for load in loads[8:]:
        load.wait()
    for chunk in range(half):
        other_half = half + chunk
        for shift in range(1 - DEPTH, DEPTH):
            level = z + shift

            @pl.when(jnp.logical_and(level >= 0, level < DEPTH))
            def _():
                lift = 4 * shift
                arrived(x_side + lift, other_half, x_sem.at[level, other_half])
                arrived(y_side + lift, chunk, y_sem.at[level, chunk])
                if abs(shift) == 1:
                    arrived(x_side + lift, chunk, x_sem.at[level, chunk])
                    arrived(y_side + lift, other_half, y_sem.at[level, other_half])
                    way = 0 if shift < 0 else 1
                    arrived(corner + lift, chunk, zc_sem.at[way, chunk])
                    arrived(corner + lift, other_half, zc_sem.at[way, other_half])
                elif shift != 0:
                    arrived(corner + lift, chunk, yd_sem.at[level, chunk])
                    arrived(corner + lift, other_half, xd_sem.at[level, chunk])

    for chunk in range(CHUNKS):
        for origin in range(SHARE):
            held = fold[origin, chunk * per_chunk + data].astype(jnp.int32).astype(jnp.float32)
            scales[chunk, origin] = jnp.exp2(held)

    wide = lax.broadcasted_iota(jnp.int32, (BLOCK_IN, 128), 1) >= 64

    def parts_of(folded):
        top = folded.astype(jnp.bfloat16).astype(jnp.float32)
        return jnp.where(wide, folded - top, top).astype(jnp.bfloat16)

    def apply_pair(p, carry):
        acc_one, acc_two = carry
        chunk = p // data
        group = lax.rem(p, data) // GROUP
        steps = fold[:, p + chunk].astype(jnp.int32).astype(jnp.float32)
        values = (steps * scales[chunk, :, pl.ds(group, 1), :]).reshape(BLOCK_IN, 128)
        turned = pltpu.roll(values, 64, 1)
        one = parts_of(jnp.where(wide, turned, values))
        two = parts_of(jnp.where(wide, values, turned))
        cols = pl.ds(pl.multiple_of(p * BLOCK_IN, BLOCK_IN), BLOCK_IN)
        acc_one = acc_one + jnp.dot(rows[:, cols], one, preferred_element_type=jnp.float32)
        cols = pl.ds(pl.multiple_of((p + half_blocks) * BLOCK_IN, BLOCK_IN), BLOCK_IN)
        acc_two = acc_two + jnp.dot(rows[:, cols], two, preferred_element_type=jnp.float32)
        return acc_one, acc_two

    zero = jnp.zeros((rows.shape[0], 128), jnp.float32)
    split = blocks_in - half_blocks
    acc_one, acc_two = lax.fori_loop(0, split, apply_pair, (zero, zero), unroll=4)
    sums_in = acc_one + acc_two
    sums_in, sums_out = lax.fori_loop(split, half_blocks, apply_pair, (sums_in, zero), unroll=4)
    for side, acc in enumerate((sums_in, sums_out)):
        turned = acc.T
        summed = turned[:64] + turned[64:]
        proj[0, side] = summed[:32]
        proj[1, side] = summed[32:]
    swap = pltpu.make_async_remote_copy(
        src_ref=proj.at[partner],
        dst_ref=other,
        send_sem=proj_sem.at[0],
        recv_sem=proj_sem.at[1],
        device_id={"tensor": partner},
        device_id_type=MESH,
    )
    swap.start()

    tokens = rows.shape[0]
    own_ids = ids_ref[...] - me * 4
    signs = []
    for slot in range(2):
        weight = jnp.zeros((1, tokens), jnp.float32)
        for k, sign in ((2 * slot, 1.0), (2 * slot + 1, -1.0)):
            count = jnp.full((1, tokens), lengths_ref[k], jnp.int32).astype(jnp.float32)
            weight = weight + jnp.where(own_ids == k, sign / count, 0.0)
        signs.append(weight)

    swap.wait()
    full = proj[core] + other[...]
    scores = (full[0] * full[1]).reshape(4, RANK, tokens).sum(axis=1)
    scores_ref[...] = scores
    parts = [
        jnp.broadcast_to(jnp.sum(scores * weight, axis=1, keepdims=True), (4, 128))
        for weight in signs
    ]
    slots[me] = jnp.concatenate(parts, axis=0)

    def slot_copy(step):
        target = lax.rem(me + step, SHARE)
        return pltpu.make_async_remote_copy(
            src_ref=slots.at[me],
            dst_ref=slots.at[me],
            send_sem=slot_send.at[step],
            recv_sem=slot_recv.at[step],
            device_id={"train": target},
            device_id_type=MESH,
        )

    for step in range(1, SHARE):
        slot_copy(step).start()
    for index, (conds, chunk) in enumerate(pending):

        @pl.when(functools.reduce(jnp.logical_and, conds))
        def _():
            copy_of(me, chunk, index, x_sem.at[0, 0], x_side).wait_send()

    for step in range(1, SHARE):
        origin = lax.rem(me + SHARE - step, SHARE)
        pltpu.make_async_remote_copy(
            src_ref=slots.at[origin],
            dst_ref=slots.at[origin],
            send_sem=slot_send.at[step],
            recv_sem=slot_recv.at[step],
            device_id={"train": origin},
            device_id_type=MESH,
        ).wait_recv()
        slot_copy(step).wait_send()

    row = lax.broadcasted_iota(jnp.int32, (4, 128), 0)
    lane = lax.broadcasted_iota(jnp.int32, (4, 128), 1)
    for own in range(2):
        value = jnp.zeros((4, 128), jnp.float32)
        for k in range(2 * SHARE):
            same = jnp.full((4, 128), pair_ids_ref[k], jnp.int32) == me * 2 + own
            value = value + jnp.where(same, slots[k // 2, 4 * (k % 2) : 4 * (k % 2) + 4], 0.0)
        line = jnp.sum(jnp.where(row == lane, value, 0.0), axis=0, keepdims=True)
        pairs_ref[own : own + 1] = line[:, :4]


def fused(
    activations,
    out_grads,
    basis_in,
    basis_out,
    eigen_in,
    eigen_out,
    query_in,
    query_out,
    response_ids,
    lengths,
    pair_ids,
):
    tokens, hidden = activations.shape
    total = hidden + out_grads.shape[1]
    blocks = total // BLOCK_IN
    share = basis_in.shape[0]
    vmem = pl.BlockSpec(memory_space=pltpu.VMEM)
    smem = pl.BlockSpec(memory_space=pltpu.SMEM)
    scores, pair_scores = pl.pallas_call(
        fused_kernel,
        out_shape=(
            jax.ShapeDtypeStruct((4, tokens), jnp.float32),
            jax.ShapeDtypeStruct((2, 4), jnp.float32),
        ),
        in_specs=[pl.BlockSpec(memory_space=pl.ANY)] * 8 + [vmem, smem, smem],
        out_specs=(vmem, vmem),
        scratch_shapes=[
            pltpu.VMEM((tokens, total), jnp.bfloat16),
            pltpu.VMEM((share, total), jnp.bfloat16),
            pltpu.VMEM((1, total), jnp.float32),
            pltpu.VMEM((128, total), jnp.bfloat16),
            pltpu.VMEM((SHARE, blocks // 2 + CHUNKS, share, 128), jnp.int16),
            pltpu.VMEM((CHUNKS, SHARE, share, 128), jnp.float32),
            pltpu.VMEM((2, 2, 32, tokens), jnp.float32),
            pltpu.VMEM((2, 32, tokens), jnp.float32),
            pltpu.VMEM((SHARE, 8, 128), jnp.float32),
            pltpu.SemaphoreType.DMA((10,)),
            pltpu.SemaphoreType.DMA((40 * CHUNKS,)),
            pltpu.SemaphoreType.DMA((2, DEPTH - 1, CHUNKS)),
            pltpu.SemaphoreType.DMA((DEPTH, CHUNKS)),
            pltpu.SemaphoreType.DMA((DEPTH, CHUNKS)),
            pltpu.SemaphoreType.DMA((DEPTH, CHUNKS // 2)),
            pltpu.SemaphoreType.DMA((DEPTH, CHUNKS // 2)),
            pltpu.SemaphoreType.DMA((2, CHUNKS)),
            pltpu.SemaphoreType.DMA((2,)),
            pltpu.SemaphoreType.DMA((SHARE,)),
            pltpu.SemaphoreType.DMA((SHARE,)),
        ],
        compiler_params=pltpu.CompilerParams(
            collective_id=0, has_side_effects=True, vmem_limit_bytes=60 * 1024 * 1024
        ),
    )(
        activations,
        out_grads,
        basis_in,
        basis_out,
        eigen_in.reshape(1, -1),
        eigen_out.reshape(1, -1),
        query_in.T,
        query_out.T,
        response_ids.reshape(1, -1),
        lengths,
        pair_ids,
    )
    return scores.T, pair_scores


def solution(mesh):
    sizes = (mesh.shape["groups"], mesh.shape["train"], mesh.shape["tensor"])
    body = fused if sizes == (1, 16, 2) else shards
    return jax.shard_map(
        body,
        mesh=mesh,
        in_specs=(
            P(("groups", "train"), "tensor"),
            P(("groups", "train"), "tensor"),
            P("train", "tensor"),
            P("train", "tensor"),
            P("tensor"),
            P("tensor"),
            P("tensor", None),
            P("tensor", None),
            P(("groups", "train")),
            P(("groups", "train")),
            P("groups"),
        ),
        out_specs=(P(("groups", "train"), "tensor"), P(("groups", "train"), "tensor")),
        check_vma=False,
    )
```

```python
import functools

import jax
import jax.numpy as jnp
from jax import lax
from jax.experimental import pallas as pl
from jax.experimental.pallas import tpu as pltpu
from jax.sharding import PartitionSpec as P

MESH = pl.DeviceIdType.MESH

BLOCK_IN = 256
BLOCK_OUT = 256
RANK = 8
QUERIES = 8


def apply_fn(token_rows, fetched):
    return jnp.einsum(
        "tnk,nkm->tm",
        token_rows,
        fetched,
        precision=lax.Precision.HIGHEST,
        preferred_element_type=jnp.float32,
    )


def fold_local(basis, eigen, query, blocks, block_order):
    own_rows = basis.shape[0]
    scaled = (query.astype(jnp.float32) / eigen[:, None]).reshape(
        blocks, block_order, query.shape[1]
    )
    basis_part = basis.astype(jnp.float32).reshape(own_rows, blocks, block_order)
    return jnp.einsum("knj,njm->nkm", basis_part, scaled, precision=lax.Precision.HIGHEST)


def shards(
    activations,
    out_grads,
    basis_in,
    basis_out,
    eigen_in,
    eigen_out,
    query_in,
    query_out,
    response_ids,
    lengths,
    pair_ids,
):
    tok_rows = activations.shape[0]
    hidden_cols = activations.shape[1]
    feature_cols = out_grads.shape[1]
    blocks_in = hidden_cols // BLOCK_IN
    blocks_out = feature_cols // BLOCK_OUT
    rows_in = activations.reshape(tok_rows, blocks_in, BLOCK_IN)
    rows_out = out_grads.reshape(tok_rows, blocks_out, BLOCK_OUT)
    folded_in = fold_local(basis_in, eigen_in, query_in, blocks_in, BLOCK_IN)
    folded_out = fold_local(basis_out, eigen_out, query_out, blocks_out, BLOCK_OUT)
    proj_in = apply_fn(rows_in, lax.all_gather(folded_in, "train", axis=1, tiled=True))
    proj_out = apply_fn(rows_out, lax.all_gather(folded_out, "train", axis=1, tiled=True))
    proj_in, proj_out = lax.psum((proj_in, proj_out), "tensor")
    scores = (proj_in * proj_out).reshape(tok_rows, QUERIES, RANK).sum(axis=2)
    per_device = QUERIES // lax.axis_size("tensor")
    scores = lax.dynamic_slice_in_dim(scores, lax.axis_index("tensor") * per_device, per_device, 1)
    resp_dev = lengths.shape[0]
    local_ids = response_ids - lax.axis_index("train") * resp_dev
    member = (local_ids[None, :] == jnp.arange(resp_dev, dtype=jnp.int32)[:, None]).astype(
        jnp.float32
    )
    resp_sums = jnp.dot(member, scores, precision=lax.Precision.HIGHEST)
    averages = resp_sums / lengths.astype(jnp.float32)[:, None]
    slot_values = averages[0::2] - averages[1::2]
    every_slot = lax.all_gather(slot_values, "train", axis=0, tiled=True)
    pair_dev = slot_values.shape[0]
    own_pairs = lax.axis_index("train") * pair_dev + jnp.arange(pair_dev, dtype=jnp.int32)
    selector = (pair_ids[None, :] == own_pairs[:, None]).astype(jnp.float32)
    pair_scores = jnp.dot(selector, every_slot, precision=lax.Precision.HIGHEST)
    return (scores, pair_scores)


SHARE = 16
DEPTH = 4
CHUNKS = 2
GROUP = 2


def fused_kernel(
    act_hbm,
    grad_hbm,
    basis_in_hbm,
    basis_out_hbm,
    eigen_in_hbm,
    eigen_out_hbm,
    query_in_hbm,
    query_out_hbm,
    ids_ref,
    lengths_ref,
    pair_ids_ref,
    scores_ref,
    pairs_ref,
    rows,
    basis,
    eigen,
    query,
    fold,
    scales,
    proj,
    other,
    slots,
    local_sem,
    send_sem,
    z_sem,
    x_sem,
    y_sem,
    xd_sem,
    yd_sem,
    zc_sem,
    proj_sem,
    slot_send,
    slot_recv,
):
    me = lax.axis_index("train")
    core = lax.axis_index("tensor")
    x, y, z = lax.rem(me, 2), lax.rem(me // 2, 2), me // 4
    x_side = me + 1 - 2 * x
    y_side = me + 2 - 4 * y
    corner = me + 3 - 2 * x - 4 * y
    partner = 1 - core
    hidden = act_hbm.shape[1]
    total = rows.shape[1]
    blocks_in = hidden // BLOCK_IN
    blocks = total // BLOCK_IN
    half_blocks = blocks // 2
    data = half_blocks // CHUNKS
    per_chunk = data + 1
    half = CHUNKS // 2

    barrier = pltpu.get_barrier_semaphore()
    for step in range(1, SHARE):
        pl.semaphore_signal(
            barrier, inc=1, device_id={"train": lax.rem(me + step, SHARE)}, device_id_type=MESH
        )
    pl.semaphore_signal(barrier, inc=1, device_id={"tensor": partner}, device_id_type=MESH)

    first, second = pl.ds(0, hidden), pl.ds(hidden, total - hidden)
    loads = []
    pairs = [
        (basis_in_hbm, basis.at[:, first]),
        (basis_out_hbm, basis.at[:, second]),
        (eigen_in_hbm, eigen.at[:, first]),
        (eigen_out_hbm, eigen.at[:, second]),
        (query_in_hbm, query.at[pl.ds(0, 64), first]),
        (query_out_hbm, query.at[pl.ds(0, 64), second]),
        (query_in_hbm, query.at[pl.ds(64, 64), first]),
        (query_out_hbm, query.at[pl.ds(64, 64), second]),
        (act_hbm, rows.at[:, first]),
        (grad_hbm, rows.at[:, second]),
    ]
    for i, (a, b) in enumerate(pairs):
        loads.append(pltpu.make_async_copy(a, b, local_sem.at[i]))
    for load in loads[:8]:
        load.start()
    for load in loads[:8]:
        load.wait()
    for load in loads[8:]:
        load.start()

    upper = lax.broadcasted_iota(jnp.int32, (16, 128), 1) >= 64
    row_of = lax.broadcasted_iota(jnp.int32, (16, 128), 0)

    def fold_block(b):
        cols = pl.ds(pl.multiple_of(b * BLOCK_IN, BLOCK_IN), BLOCK_IN)
        scaled = basis[:, cols].astype(jnp.float32) * (1.0 / eigen[:, cols])
        high = scaled.astype(jnp.bfloat16)
        low = (scaled - high.astype(jnp.float32)).astype(jnp.bfloat16)
        dims = (((1,), (1,)), ((), ()))
        both = lax.dot_general(
            jnp.concatenate([high, low], axis=0),
            query[:, cols],
            dims,
            preferred_element_type=jnp.float32,
        )
        return both[:16] + both[16:]

    def fold_group(chunk, r, exponents):
        values = []
        for i in range(GROUP):
            b = chunk * data + r * GROUP + i
            values.append(jnp.where(upper, fold_block(b + half_blocks), fold_block(b)))
        largest = functools.reduce(jnp.maximum, [jnp.abs(v) for v in values])
        largest = jnp.maximum(jnp.max(largest, axis=0, keepdims=True), 1e-30)
        exponent = jnp.floor(jnp.log2(largest)) - 14.0
        inverse = jnp.exp2(-exponent)
        for i, v in enumerate(values):
            steps = jnp.clip(jnp.round(v * inverse), -32767.0, 32767.0)
            tile = chunk * per_chunk + r * GROUP + i
            fold[me, tile] = steps.astype(jnp.int32).astype(jnp.int16)
        return jnp.where(row_of == r, exponent, exponents)

    pending = []

    def copy_of(origin, chunk, index, sem, target):
        ref = fold.at[origin, pl.ds(chunk * per_chunk, per_chunk)]
        return pltpu.make_async_remote_copy(
            src_ref=ref,
            dst_ref=ref,
            send_sem=send_sem.at[index],
            recv_sem=sem,
            device_id={"train": target},
            device_id_type=MESH,
        )

    def send(when, origin, chunk, sem, target):
        copy = copy_of(origin, chunk, len(pending), sem, target)
        pending.append(((when,), chunk))
        copy.start()

    def send_if(when, cond, origin, chunk, sem, target):
        copy = copy_of(origin, chunk, len(pending), sem, target)
        pending.append(((when, cond), chunk))

        @pl.when(cond)
        def _():
            copy.start()

    def arrived(origin, chunk, sem):
        copy_of(origin, chunk, 0, sem, x_side).wait_recv()

    always = z >= 0
    up, down = z < DEPTH - 1, z > 0

    for chunk in range(CHUNKS):
        exponents = lax.fori_loop(
            0,
            data // GROUP,
            functools.partial(fold_group, chunk),
            jnp.zeros((16, 128), jnp.float32),
            unroll=3,
        )
        fold[me, chunk * per_chunk + data] = exponents.astype(jnp.int32).astype(jnp.int16)
        if chunk == 0:
            pl.semaphore_wait(barrier, SHARE)
        send_if(always, up, me, chunk, z_sem.at[0, 0, chunk], me + 4)
        send_if(always, down, me, chunk, z_sem.at[1, 0, chunk], me - 4)
        send(always, me, chunk, x_sem.at[z, chunk], x_side)
        send(always, me, chunk, y_sem.at[z, chunk], y_side)

    def column(step):
        for chunk in range(CHUNKS):
            for way, shift in ((0, -step), (1, step)):
                when = z + shift >= 0 if shift < 0 else z + shift < DEPTH

                @pl.when(when)
                def _():
                    origin = me + 4 * shift
                    arrived(origin, chunk, z_sem.at[way, step - 1, chunk])
                    if step < DEPTH - 1:
                        cond, target = (up, me + 4) if way == 0 else (down, me - 4)
                        send_if(when, cond, origin, chunk, z_sem.at[way, step, chunk], target)
                    send(when, origin, chunk, x_sem.at[z + shift, chunk], x_side)
                    send(when, origin, chunk, y_sem.at[z + shift, chunk], y_side)

    def across(step):
        shifts = (0,) if step == 0 else (-step, step)
        for chunk in range(half):
            for shift in shifts:
                when = z + shift >= 0 if shift < 0 else z + shift < DEPTH

                @pl.when(when)
                def _():
                    level = z + shift
                    origin = x_side + 4 * shift
                    arrived(origin, chunk, x_sem.at[level, chunk])
                    send(when, origin, chunk, yd_sem.at[level, chunk], y_side)
                    origin = y_side + 4 * shift
                    arrived(origin, half + chunk, y_sem.at[level, half + chunk])
                    send(when, origin, half + chunk, xd_sem.at[level, chunk], x_side)

    def corner_share():
        for chunk in range(CHUNKS):
            if chunk < half:
                arrived(corner, chunk, yd_sem.at[z, chunk])
            else:
                arrived(corner, chunk, xd_sem.at[z, chunk - half])
            send_if(always, up, corner, chunk, zc_sem.at[0, chunk], me + 4)
            send_if(always, down, corner, chunk, zc_sem.at[1, chunk], me - 4)

    column(1)
    across(0)
    column(2)
    corner_share()
    column(3)
    across(2)
    across(3)

    for load in loads[8:]:
        load.wait()
    for chunk in range(half):
        other_half = half + chunk
        for shift in range(1 - DEPTH, DEPTH):
            level = z + shift

            @pl.when(jnp.logical_and(level >= 0, level < DEPTH))
            def _():
                lift = 4 * shift
                arrived(x_side + lift, other_half, x_sem.at[level, other_half])
                arrived(y_side + lift, chunk, y_sem.at[level, chunk])
                if abs(shift) == 1:
                    arrived(x_side + lift, chunk, x_sem.at[level, chunk])
                    arrived(y_side + lift, other_half, y_sem.at[level, other_half])
                    way = 0 if shift < 0 else 1
                    arrived(corner + lift, chunk, zc_sem.at[way, chunk])
                    arrived(corner + lift, other_half, zc_sem.at[way, other_half])
                elif shift != 0:
                    arrived(corner + lift, chunk, yd_sem.at[level, chunk])
                    arrived(corner + lift, other_half, xd_sem.at[level, chunk])

    for chunk in range(CHUNKS):
        for origin in range(SHARE):
            held = fold[origin, chunk * per_chunk + data].astype(jnp.int32).astype(jnp.float32)
            scales[chunk, origin] = jnp.exp2(held)

    wide = lax.broadcasted_iota(jnp.int32, (BLOCK_IN, 128), 1) >= 64

    def parts_of(folded):
        top = folded.astype(jnp.bfloat16).astype(jnp.float32)
        return jnp.where(wide, folded - top, top).astype(jnp.bfloat16)

    def apply_pair(p, carry):
        acc_one, acc_two = carry
        chunk = p // data
        group = lax.rem(p, data) // GROUP
        steps = fold[:, p + chunk].astype(jnp.int32).astype(jnp.float32)
        values = (steps * scales[chunk, :, pl.ds(group, 1), :]).reshape(BLOCK_IN, 128)
        turned = pltpu.roll(values, 64, 1)
        one = parts_of(jnp.where(wide, turned, values))
        two = parts_of(jnp.where(wide, values, turned))
        cols = pl.ds(pl.multiple_of(p * BLOCK_IN, BLOCK_IN), BLOCK_IN)
        acc_one = acc_one + jnp.dot(rows[:, cols], one, preferred_element_type=jnp.float32)
        cols = pl.ds(pl.multiple_of((p + half_blocks) * BLOCK_IN, BLOCK_IN), BLOCK_IN)
        acc_two = acc_two + jnp.dot(rows[:, cols], two, preferred_element_type=jnp.float32)
        return acc_one, acc_two

    zero = jnp.zeros((rows.shape[0], 128), jnp.float32)
    split = blocks_in - half_blocks
    acc_one, acc_two = lax.fori_loop(0, split, apply_pair, (zero, zero), unroll=10)
    sums_in = acc_one + acc_two
    sums_in, sums_out = lax.fori_loop(split, half_blocks, apply_pair, (sums_in, zero), unroll=8)
    for side, acc in enumerate((sums_in, sums_out)):
        turned = acc.T
        summed = turned[:64] + turned[64:]
        proj[0, side] = summed[:32]
        proj[1, side] = summed[32:]
    swap = pltpu.make_async_remote_copy(
        src_ref=proj.at[partner],
        dst_ref=other,
        send_sem=proj_sem.at[0],
        recv_sem=proj_sem.at[1],
        device_id={"tensor": partner},
        device_id_type=MESH,
    )
    swap.start()

    tokens = rows.shape[0]
    own_ids = ids_ref[...] - me * 4
    signs = []
    for slot in range(2):
        weight = jnp.zeros((1, tokens), jnp.float32)
        for k, sign in ((2 * slot, 1.0), (2 * slot + 1, -1.0)):
            count = jnp.full((1, tokens), lengths_ref[k], jnp.int32).astype(jnp.float32)
            weight = weight + jnp.where(own_ids == k, sign / count, 0.0)
        signs.append(weight)

    swap.wait()
    full = proj[core] + other[...]
    scores = (full[0] * full[1]).reshape(4, RANK, tokens).sum(axis=1)
    scores_ref[...] = scores
    parts = [
        jnp.broadcast_to(jnp.sum(scores * weight, axis=1, keepdims=True), (4, 128))
        for weight in signs
    ]
    slots[me] = jnp.concatenate(parts, axis=0)

    def slot_copy(step):
        target = lax.rem(me + step, SHARE)
        return pltpu.make_async_remote_copy(
            src_ref=slots.at[me],
            dst_ref=slots.at[me],
            send_sem=slot_send.at[step],
            recv_sem=slot_recv.at[step],
            device_id={"train": target},
            device_id_type=MESH,
        )

    for step in range(1, SHARE):
        slot_copy(step).start()
    for index, (conds, chunk) in enumerate(pending):

        @pl.when(functools.reduce(jnp.logical_and, conds))
        def _():
            copy_of(me, chunk, index, x_sem.at[0, 0], x_side).wait_send()

    for step in range(1, SHARE):
        origin = lax.rem(me + SHARE - step, SHARE)
        pltpu.make_async_remote_copy(
            src_ref=slots.at[origin],
            dst_ref=slots.at[origin],
            send_sem=slot_send.at[step],
            recv_sem=slot_recv.at[step],
            device_id={"train": origin},
            device_id_type=MESH,
        ).wait_recv()
        slot_copy(step).wait_send()

    row = lax.broadcasted_iota(jnp.int32, (4, 128), 0)
    lane = lax.broadcasted_iota(jnp.int32, (4, 128), 1)
    for own in range(2):
        value = jnp.zeros((4, 128), jnp.float32)
        for k in range(2 * SHARE):
            same = jnp.full((4, 128), pair_ids_ref[k], jnp.int32) == me * 2 + own
            value = value + jnp.where(same, slots[k // 2, 4 * (k % 2) : 4 * (k % 2) + 4], 0.0)
        line = jnp.sum(jnp.where(row == lane, value, 0.0), axis=0, keepdims=True)
        pairs_ref[own : own + 1] = line[:, :4]


def fused(
    activations,
    out_grads,
    basis_in,
    basis_out,
    eigen_in,
    eigen_out,
    query_in,
    query_out,
    response_ids,
    lengths,
    pair_ids,
):
    tokens, hidden = activations.shape
    total = hidden + out_grads.shape[1]
    blocks = total // BLOCK_IN
    share = basis_in.shape[0]
    vmem = pl.BlockSpec(memory_space=pltpu.VMEM)
    smem = pl.BlockSpec(memory_space=pltpu.SMEM)
    scores, pair_scores = pl.pallas_call(
        fused_kernel,
        out_shape=(
            jax.ShapeDtypeStruct((4, tokens), jnp.float32),
            jax.ShapeDtypeStruct((2, 4), jnp.float32),
        ),
        in_specs=[pl.BlockSpec(memory_space=pl.ANY)] * 8 + [vmem, smem, smem],
        out_specs=(vmem, vmem),
        scratch_shapes=[
            pltpu.VMEM((tokens, total), jnp.bfloat16),
            pltpu.VMEM((share, total), jnp.bfloat16),
            pltpu.VMEM((1, total), jnp.float32),
            pltpu.VMEM((128, total), jnp.bfloat16),
            pltpu.VMEM((SHARE, blocks // 2 + CHUNKS, share, 128), jnp.int16),
            pltpu.VMEM((CHUNKS, SHARE, share, 128), jnp.float32),
            pltpu.VMEM((2, 2, 32, tokens), jnp.float32),
            pltpu.VMEM((2, 32, tokens), jnp.float32),
            pltpu.VMEM((SHARE, 8, 128), jnp.float32),
            pltpu.SemaphoreType.DMA((10,)),
            pltpu.SemaphoreType.DMA((40 * CHUNKS,)),
            pltpu.SemaphoreType.DMA((2, DEPTH - 1, CHUNKS)),
            pltpu.SemaphoreType.DMA((DEPTH, CHUNKS)),
            pltpu.SemaphoreType.DMA((DEPTH, CHUNKS)),
            pltpu.SemaphoreType.DMA((DEPTH, CHUNKS // 2)),
            pltpu.SemaphoreType.DMA((DEPTH, CHUNKS // 2)),
            pltpu.SemaphoreType.DMA((2, CHUNKS)),
            pltpu.SemaphoreType.DMA((2,)),
            pltpu.SemaphoreType.DMA((SHARE,)),
            pltpu.SemaphoreType.DMA((SHARE,)),
        ],
        compiler_params=pltpu.CompilerParams(
            collective_id=0, has_side_effects=True, vmem_limit_bytes=60 * 1024 * 1024
        ),
    )(
        activations,
        out_grads,
        basis_in,
        basis_out,
        eigen_in.reshape(1, -1),
        eigen_out.reshape(1, -1),
        query_in.T,
        query_out.T,
        response_ids.reshape(1, -1),
        lengths,
        pair_ids,
    )
    return scores.T, pair_scores


def solution(mesh):
    sizes = (mesh.shape["groups"], mesh.shape["train"], mesh.shape["tensor"])
    body = fused if sizes == (1, 16, 2) else shards
    return jax.shard_map(
        body,
        mesh=mesh,
        in_specs=(
            P(("groups", "train"), "tensor"),
            P(("groups", "train"), "tensor"),
            P("train", "tensor"),
            P("train", "tensor"),
            P("tensor"),
            P("tensor"),
            P("tensor", None),
            P("tensor", None),
            P(("groups", "train")),
            P(("groups", "train")),
            P("groups"),
        ),
        out_specs=(P(("groups", "train"), "tensor"), P(("groups", "train"), "tensor")),
        check_vma=False,
    )
```
